32 devices in a mesh: dp: 8 (over z, core), node: 4 (over y, x).
Axes of the slice: x: 2, y: 2, z: 4, core: 2. Of those that a mesh axis runs over, the one named last changes fastest.
Arguments:
- inputs: bfloat16 [4096, 4096], P(('dp', 'node')), may hold values from -6 to 6
- queries: bfloat16 [4096, 4096], P(('dp', 'node')), may hold values from -130 to 130
- keys: bfloat16 [4096, 512], P(('dp', 'node')), may hold values from -6 to 6
- attention_gradient: bfloat16 [4096, 4096], P(('dp', 'node')), may hold values from -6 to 6
- value_matrix: bfloat16 [4096, 512], P('node'), may hold values from -0.09375 to 0.09375
Outputs:
- key_gradient: bfloat16 [4096, 512], P(('dp', 'node'))
- value_weight_gradient: float32 [4096, 512], P(('node', 'dp'))
The draws below stay inside these ranges and needn't reach their ends.
All inputs are finite; a program needn't handle non-finite values.
Results may differ from the reference program's by a relative error of at most 0.009.
Values may be sent and summed in bfloat16 or wider, within the bound.
No kernel may reach another device: no remote copies, remote signals or barrier semaphores. Data moves between devices by JAX's collectives and lax.ppermute only.
A program may use at most 64 MiB of HBM per device.

```python
import jax
import jax.numpy as jnp
from jax import lax

MODEL_WIDTH = 4096
QUERY_HEADS = 32
KEY_VALUE_HEADS = 4
HEAD_SIZE = 128
TOK_DEV = 128
TOKEN_TOTAL = 4096
N_DP = 8
N_NODE = 4


def shared_keys(key):
    starting_keys = jax.random.normal(jax.random.fold_in(key, 11), (TOKEN_TOTAL, KEY_VALUE_HEADS * HEAD_SIZE), jnp.float32)
    return jnp.clip(starting_keys, -5.0, 5.0)


def draw_keys(key, part):
    starting_keys = shared_keys(key)
    return starting_keys.astype(jnp.bfloat16)


def draw_queries(key, part):
    key = jax.random.fold_in(key, 5)
    drawn_draw = jnp.clip(jax.random.normal(key, (TOKEN_TOTAL, QUERY_HEADS * HEAD_SIZE), jnp.float32), -5.0, 5.0)
    return drawn_draw.astype(jnp.bfloat16)


def strengthened(entries, own_key, source, target, blocks, factor):
    owner, partner = [(jnp.arange(entries.shape[axis_at]) // (entries.shape[axis_at] // blocks)).reshape([-1 if axis == axis_at else 1 for axis in range(entries.ndim)]) for axis_at in (source, target)]
    chosen = jax.random.permutation(own_key, blocks)[partner]
    strong = (owner == chosen) | (owner == (partner + blocks // 2) % blocks)
    return jnp.where(strong, factor * entries, entries)


def block_scale(own_key, extent, split, low, top_value):
    def one(position, blocks):
        heights = jax.random.uniform(jax.random.fold_in(jax.random.fold_in(own_key, 6), position), (blocks,), jnp.float32, low / len(split), top_value / len(split))
        return jnp.repeat(jnp.exp(heights), extent[position] // blocks).reshape((-1,) + (1,) * (len(extent) - position - 1))

    loudness = one(*split[0])
    for cut in split[1:]:
        loudness = loudness * one(*cut)
    return loudness


def bell_draw(rng, extent, deviation, limit, cuts=(), dtype=jnp.bfloat16):
    entries = deviation * jax.random.normal(rng, extent, jnp.float32)
    if cuts:
        entries = entries * block_scale(rng, extent, cuts, -0.22, 0.18)
    return jnp.clip(entries, -limit, limit).astype(dtype)


def gaussian_with(rng, dims, spread, limit, cuts, heavy, held_as=jnp.bfloat16):
    values = spread * jax.random.normal(rng, dims, jnp.float32)
    if cuts:
        values = values * block_scale(rng, dims, cuts, -0.22, 0.18)
    return jnp.clip(strengthened(values, jax.random.fold_in(rng, 3), *heavy), -limit, limit).astype(held_as)


def setup_inputs(seed: int = 0) -> dict:
    splits = jax.random.split(jax.random.key(seed), 6)
    return {
        "inputs": gaussian_with(splits[0], (TOKEN_TOTAL, MODEL_WIDTH), 1.0, 6.0, ((0, 32),), (0, 1, 32, 2.75)),
        "queries": draw_queries(jax.random.fold_in(splits[5], 71), 0),
        "keys": draw_keys(jax.random.fold_in(splits[5], 71), 0),
        "attention_gradient": bell_draw(splits[3], (TOKEN_TOTAL, QUERY_HEADS * HEAD_SIZE), 1.0, 6.0, ((0, 32),)),
        "value_matrix": bell_draw(splits[4], (MODEL_WIDTH, KEY_VALUE_HEADS * HEAD_SIZE), MODEL_WIDTH ** -0.5, 0.09375, ((0, 4),)),
    }


def attend(queries, keys, value_tensor, attention_gradient):
    sequence_length = queries.shape[0]
    group_count = QUERY_HEADS // KEY_VALUE_HEADS
    factor = HEAD_SIZE ** -0.5
    head_queries = queries.astype(jnp.float32).reshape(sequence_length, KEY_VALUE_HEADS, group_count, HEAD_SIZE)
    head_keys = keys.astype(jnp.float32).reshape(sequence_length, KEY_VALUE_HEADS, HEAD_SIZE)
    head_values = value_tensor.astype(jnp.float32).reshape(sequence_length, KEY_VALUE_HEADS, HEAD_SIZE)
    gradient_heads = attention_gradient.astype(jnp.float32).reshape(sequence_length, KEY_VALUE_HEADS, group_count, HEAD_SIZE)
    scores = jnp.einsum("qhgd,khd->hgqk", head_queries, head_keys) * factor
    causal = jnp.arange(sequence_length)[:, None] >= jnp.arange(sequence_length)[None, :]
    scores = jnp.where(causal, scores, -1e30)
    largest = jnp.max(scores, axis=-1, keepdims=True)
    exponent = jnp.exp(scores - largest)
    attention = exponent / jnp.sum(exponent, axis=-1, keepdims=True)
    attention_low = attention.astype(jnp.bfloat16).astype(jnp.float32)
    d_attention = jnp.einsum("qhgd,khd->hgqk", gradient_heads, head_values)
    row_dots = jnp.sum(attention * d_attention, axis=-1, keepdims=True)
    d_scores = (attention * (d_attention - row_dots)).astype(jnp.bfloat16).astype(jnp.float32)
    key_gradient = (jnp.einsum("hgqk,qhgd->khd", d_scores, head_queries) * factor).astype(jnp.bfloat16)
    value_gradient = jnp.einsum("hgqk,qhgd->khd", attention_low, gradient_heads).astype(jnp.bfloat16)
    return key_gradient.reshape(sequence_length, KEY_VALUE_HEADS * HEAD_SIZE), value_gradient.reshape(sequence_length, KEY_VALUE_HEADS * HEAD_SIZE)


def reference(inputs, queries, keys, attention_gradient, value_matrix):
    sequences = inputs.shape[0] // TOK_DEV

    def shaped(array):
        return array.reshape(sequences, TOK_DEV, array.shape[1])

    def advance(running, pieces):
        rows_in, query_rows, key_rows, grad_rows = pieces
        value_tensor = jnp.dot(rows_in, value_matrix, preferred_element_type=jnp.float32).astype(jnp.bfloat16)
        key_gradient, value_gradient = attend(query_rows, key_rows, value_tensor, grad_rows)
        partial_value = jnp.dot(rows_in.T, value_gradient, preferred_element_type=jnp.float32)
        rounded = lax.optimization_barrier(partial_value.astype(jnp.bfloat16))
        return running + rounded.astype(jnp.float32), key_gradient

    initial_sum = jnp.zeros((MODEL_WIDTH, KEY_VALUE_HEADS * HEAD_SIZE), jnp.float32)
    running, key_gradient = lax.scan(advance, initial_sum, (shaped(inputs), shaped(queries), shaped(keys), shaped(attention_gradient)))
    value_weight_gradient = running / (N_DP * N_NODE)
    return key_gradient.reshape(inputs.shape[0], KEY_VALUE_HEADS * HEAD_SIZE), value_weight_gradient
```

```python
import functools

import jax
import jax.numpy as jnp
from jax import lax
from jax.experimental import pallas as pl
from jax.experimental.pallas import tpu as pltpu
from jax.sharding import PartitionSpec as P

QUERY_HEADS = 32
KEY_VALUE_HEADS = 4
HEAD_SIZE = 128
GROUP = QUERY_HEADS // KEY_VALUE_HEADS
FACTOR = HEAD_SIZE ** (-0.5)
LOG2_E = 1.4426950408889634
VMEM = pl.BlockSpec(memory_space=pltpu.VMEM)


def dot(a, b):
    return jnp.dot(a, b, preferred_element_type=jnp.float32)


def dot_nt(a, b):
    return lax.dot_general(a, b, (((1,), (1,)), ((), ())), preferred_element_type=jnp.float32)


def dot_tn(a, b):
    return lax.dot_general(a, b, (((0,), (0,)), ((), ())), preferred_element_type=jnp.float32)


def head(ref, h):
    return ref[:, h * HEAD_SIZE : (h + 1) * HEAD_SIZE]


def softmax_kernel(q_ref, k_ref, g_ref, dv_ref, p_ref):
    tokens = q_ref.shape[0]
    key = k_ref[...]
    seen = lax.broadcasted_iota(jnp.int32, (tokens, tokens), 0) <= lax.broadcasted_iota(
        jnp.int32, (tokens, tokens), 1
    )
    total = None
    for h in range(GROUP):
        scores = jnp.where(seen, dot_nt(key, head(q_ref, h)), -1e30)
        exponent = jnp.exp2((scores - jnp.max(scores, axis=0, keepdims=True)) * (FACTOR * LOG2_E))
        attention = exponent * (1.0 / jnp.sum(exponent, axis=0, keepdims=True))
        p_ref[:, h * tokens : (h + 1) * tokens] = attention
        part = dot(attention.astype(jnp.bfloat16), head(g_ref, h))
        total = part if total is None else total + part
    dv_ref[...] = total.astype(jnp.bfloat16)


def softmax_call(queries, keys, gradient):
    tokens = queries.shape[0]
    wide = pl.BlockSpec((tokens, GROUP * HEAD_SIZE), lambda g: (0, g))
    narrow = pl.BlockSpec((tokens, HEAD_SIZE), lambda g: (0, g))
    return pl.pallas_call(
        softmax_kernel,
        grid=(KEY_VALUE_HEADS,),
        in_specs=[wide, narrow, wide],
        out_specs=[narrow, pl.BlockSpec((tokens, GROUP * tokens), lambda g: (0, g))],
        out_shape=[
            jax.ShapeDtypeStruct((tokens, KEY_VALUE_HEADS * HEAD_SIZE), jnp.bfloat16),
            jax.ShapeDtypeStruct((tokens, QUERY_HEADS * tokens), jnp.float32),
        ],
        cost_estimate=pl.CostEstimate(flops=4_000_000_000, bytes_accessed=8_000_000, transcendentals=0),
    )(queries, keys, gradient)


def key_kernel(q_ref, g_ref, p_ref, *rest):
    value_refs, out_ref = rest[:-1], rest[-1]
    tokens = q_ref.shape[0]
    value = value_refs[0][...].astype(jnp.float32)
    for ref in value_refs[1:]:
        value = value + ref[...].astype(jnp.float32)
    value = value.astype(jnp.bfloat16)
    total = None
    for h in range(GROUP):
        attention = p_ref[:, h * tokens : (h + 1) * tokens]
        d_attention = dot_nt(value, head(g_ref, h))
        row_dots = jnp.sum(attention * d_attention, axis=0, keepdims=True)
        d_scores = (attention * (d_attention - row_dots)).astype(jnp.bfloat16)
        part = dot(d_scores, head(q_ref, h))
        total = part if total is None else total + part
    out_ref[...] = (total * FACTOR).astype(jnp.bfloat16)


def key_call(queries, gradient, attention, values):
    tokens = queries.shape[0]
    wide = pl.BlockSpec((tokens, GROUP * HEAD_SIZE), lambda g: (0, g))
    narrow = pl.BlockSpec((tokens, HEAD_SIZE), lambda g: (0, g))
    return pl.pallas_call(
        key_kernel,
        grid=(KEY_VALUE_HEADS,),
        in_specs=[wide, wide, pl.BlockSpec((tokens, GROUP * tokens), lambda g: (0, g))] + [narrow] * len(values),
        out_specs=narrow,
        out_shape=jax.ShapeDtypeStruct((tokens, KEY_VALUE_HEADS * HEAD_SIZE), jnp.bfloat16),
        cost_estimate=pl.CostEstimate(flops=4_000_000_000, bytes_accessed=8_000_000, transcendentals=0),
    )(queries, gradient, attention, *values)


def values_kernel(*refs):
    n = len(refs) // 2
    weights = refs[n][...]
    for source, out in zip(refs[:n], refs[n + 1 :]):
        out[...] = dot(source[...], weights).astype(out.dtype)


def values_call(blocks, weights):
    n = len(blocks)
    shape = (blocks[0].shape[0], weights.shape[1])
    return pl.pallas_call(
        values_kernel,
        in_specs=[VMEM] * (n + 1),
        out_specs=[VMEM] * n,
        out_shape=[jax.ShapeDtypeStruct(shape, jnp.float32 if i == 0 else jnp.bfloat16) for i in range(n)],
        cost_estimate=pl.CostEstimate(flops=2_000_000_000, bytes_accessed=3_000_000, transcendentals=0),
    )(*blocks, weights)


def weight_kernel(n, place_ref, *refs):
    blocks, d_values, send_ref, keep_ref = refs[:n], refs[n : 2 * n], refs[2 * n], refs[2 * n + 1]
    rows = keep_ref.shape[1]
    core = place_ref[0]
    values = jnp.concatenate([ref[...] for ref in d_values], axis=0)
    for i in range(keep_ref.shape[0]):
        for parity, out in ((1 - core, send_ref), (core, keep_ref)):
            columns = pl.ds(pl.multiple_of((2 * i + parity) * rows, rows), rows)
            source = jnp.concatenate([ref[:, columns] for ref in blocks], axis=0)
            out[i] = dot_tn(source, values).astype(out.dtype)


def weight_call(blocks, d_values, core, owners):
    n = len(blocks)
    width = d_values[0].shape[1]
    shape = (owners // 2, blocks[0].shape[1] // owners, width)
    return pl.pallas_call(
        functools.partial(weight_kernel, n),
        in_specs=[pl.BlockSpec(memory_space=pltpu.SMEM)] + [VMEM] * (2 * n),
        out_specs=[VMEM] * 2,
        out_shape=[jax.ShapeDtypeStruct(shape, jnp.bfloat16), jax.ShapeDtypeStruct(shape, jnp.float32)],
        cost_estimate=pl.CostEstimate(flops=2_000_000_000, bytes_accessed=3_000_000, transcendentals=0),
    )(core.reshape(1), *blocks, *d_values)


def swap(array, axis, distance):
    size = lax.axis_size(axis)
    return lax.ppermute(array, axis, [(i, i ^ distance) for i in range(size)])


def per_device(inputs, queries, keys, attention_gradient, value_matrix):
    nodes, owners = lax.axis_size("node"), lax.axis_size("dp")
    node, owner = lax.axis_index("node"), lax.axis_index("dp")
    width = inputs.shape[1] // nodes

    def columns_of(other):
        return lax.dynamic_slice_in_dim(inputs, other * width, width, axis=1)

    blocks = [columns_of(node)]
    blocks += [swap(columns_of(node ^ k), "node", k) for k in range(1, nodes)]
    d_values, attention = softmax_call(queries, keys, attention_gradient)
    all_d_values = [d_values] + [swap(d_values, "node", k) for k in range(1, nodes)]
    parts = values_call(blocks, value_matrix)
    values = [parts[0]] + [swap(parts[k], "node", k) for k in range(1, nodes)]
    key_gradient = key_call(queries, attention_gradient, attention, values)

    rows = width // owners
    if rows % 16 or owners % 2:
        local = dot_tn(jnp.concatenate(blocks, axis=0), jnp.concatenate(all_d_values, axis=0))
        owned = lax.psum_scatter(local, "dp", scatter_dimension=0, tiled=True)
        return key_gradient, owned / (owners * nodes)
    core, chip, chips = owner % 2, owner // 2, owners // 2
    send, keep = weight_call(blocks, all_d_values, core, owners)
    pair = keep + swap(send, "dp", 1).astype(jnp.float32)

    def chip_rows(other):
        return lax.dynamic_index_in_dim(pair, other, axis=0, keepdims=False)

    owned = chip_rows(chip)
    for k in range(1, chips):
        owned += swap(chip_rows(chip ^ k).astype(jnp.bfloat16), "dp", 2 * k).astype(jnp.float32)
    return key_gradient, owned / (owners * nodes)


def solution(mesh):
    placed = (
        P(("dp", "node"), None),
        P(("dp", "node"), None),
        P(("dp", "node"), None),
        P(("dp", "node"), None),
        P("node", None),
    )
    return jax.shard_map(
        per_device,
        mesh=mesh,
        in_specs=placed,
        out_specs=(P(("dp", "node"), None), P(("node", "dp"), None)),
        check_vma=False,
    )
```

```python
import functools

import jax
import jax.numpy as jnp
from jax import lax
from jax.experimental import pallas as pl
from jax.experimental.pallas import tpu as pltpu
from jax.sharding import PartitionSpec as P

QUERY_HEADS = 32
KEY_VALUE_HEADS = 4
HEAD_SIZE = 128
GROUP = QUERY_HEADS // KEY_VALUE_HEADS
FACTOR = HEAD_SIZE ** (-0.5)
LOG2_E = 1.4426950408889634
VMEM = pl.BlockSpec(memory_space=pltpu.VMEM)


def dot(a, b):
    return jnp.dot(a, b, preferred_element_type=jnp.float32)


def dot_nt(a, b):
    return lax.dot_general(a, b, (((1,), (1,)), ((), ())), preferred_element_type=jnp.float32)


def dot_tn(a, b):
    return lax.dot_general(a, b, (((0,), (0,)), ((), ())), preferred_element_type=jnp.float32)


def head(ref, h):
    return ref[:, h * HEAD_SIZE : (h + 1) * HEAD_SIZE]


def stack(ref, first, count):
    return jnp.concatenate([head(ref, first + i) for i in range(count)], axis=0)


def call(kernel, out_shape, flops, arguments, in_specs=None, scratch=()):
    return pl.pallas_call(
        kernel,
        in_specs=in_specs or [VMEM] * len(arguments),
        out_specs=[VMEM] * len(out_shape),
        out_shape=out_shape,
        scratch_shapes=scratch,
        compiler_params=pltpu.CompilerParams(vmem_limit_bytes=40 << 20),
        cost_estimate=pl.CostEstimate(flops=flops, bytes_accessed=1_000_000, transcendentals=0),
    )(*arguments)


def struct(shape, dtype):
    return jax.ShapeDtypeStruct(shape, dtype)


def pack_kernel(nodes, source_ref, *refs):
    outs, sems = refs[:nodes], refs[nodes]
    node = lax.axis_index("node")
    width = outs[0].shape[1]
    copies = []
    for k in (*range(1, nodes), 0):
        columns = pl.ds(pl.multiple_of((node ^ k) * width, width), width)
        copies.append(pltpu.make_async_copy(source_ref.at[:, columns], outs[k], sems.at[k]))
        copies[-1].start()
    for copy in copies:
        copy.wait()


def pack_call(inputs, nodes):
    shape = (inputs.shape[0], inputs.shape[1] // nodes)
    return call(
        functools.partial(pack_kernel, nodes),
        [struct(shape, inputs.dtype)] * nodes,
        500_000_000,
        (inputs,),
        [pl.BlockSpec(memory_space=pl.ANY)],
        [pltpu.SemaphoreType.DMA((nodes,))],
    )


def softmax_kernel(q_ref, k_ref, g_ref, dv_ref, p_ref):
    tokens = q_ref.shape[0]
    wide = (tokens, GROUP * tokens)
    query = lax.broadcasted_iota(jnp.int32, wide, 1) % tokens
    seen = lax.broadcasted_iota(jnp.int32, wide, 0) <= query
    for g in range(KEY_VALUE_HEADS):
        scores = jnp.where(seen, dot_nt(head(k_ref, g), stack(q_ref, g * GROUP, GROUP)), -1e30)
        exponent = jnp.exp2((scores - jnp.max(scores, axis=0, keepdims=True)) * (FACTOR * LOG2_E))
        attention = exponent * (1.0 / jnp.sum(exponent, axis=0, keepdims=True))
        p_ref[:, g * wide[1] : (g + 1) * wide[1]] = attention
        d_values = dot(attention.astype(jnp.bfloat16), stack(g_ref, g * GROUP, GROUP))
        dv_ref[:, g * HEAD_SIZE : (g + 1) * HEAD_SIZE] = d_values.astype(jnp.bfloat16)


def softmax_call(queries, keys, gradient):
    tokens = queries.shape[0]
    outs = [struct(keys.shape, jnp.bfloat16), struct((tokens, QUERY_HEADS * tokens), jnp.float32)]
    return call(softmax_kernel, outs, 3_000_000_000, (queries, keys, gradient))


def key_kernel(q_ref, g_ref, p_ref, *rest):
    value_refs, out_ref = rest[:-1], rest[-1]
    wide = GROUP * q_ref.shape[0]
    for g in range(KEY_VALUE_HEADS):
        value = sum(head(ref, g).astype(jnp.float32) for ref in value_refs).astype(jnp.bfloat16)
        attention = p_ref[:, g * wide : (g + 1) * wide]
        d_attention = dot_nt(value, stack(g_ref, g * GROUP, GROUP))
        row_dots = jnp.sum(attention * d_attention, axis=0, keepdims=True)
        d_scores = (attention * (d_attention - row_dots)).astype(jnp.bfloat16)
        gradient = dot(d_scores, stack(q_ref, g * GROUP, GROUP)) * FACTOR
        out_ref[:, g * HEAD_SIZE : (g + 1) * HEAD_SIZE] = gradient.astype(jnp.bfloat16)


def key_call(queries, gradient, attention, values):
    outs = [struct(values[0].shape, jnp.bfloat16)]
    return call(key_kernel, outs, 2_500_000_000, (queries, gradient, attention, *values))[0]


def values_kernel(*refs):
    n = len(refs) // 2
    weights = refs[n][...]
    for source, out in zip(refs[:n], refs[n + 1 :]):
        out[...] = dot(source[...], weights).astype(out.dtype)


def values_call(blocks, weights):
    n = len(blocks)
    shape = (blocks[0].shape[0], weights.shape[1])
    outs = [struct(shape, jnp.float32 if i == 0 else jnp.bfloat16) for i in range(n)]
    return call(values_kernel, outs, 1_500_000_000, (*blocks, weights))


def weight_kernel(n, other, owners, *refs):
    blocks, d_values, out_ref = refs[:n], refs[n : 2 * n], refs[-1]
    chips, rows, width = out_ref.shape
    core = (lax.axis_index("dp") + other) % 2
    columns = [pl.ds(pl.multiple_of((2 * i + core) * rows, rows), rows) for i in range(chips)]
    source = jnp.concatenate(
        [jnp.concatenate([ref[:, c] for c in columns], axis=1) for ref in blocks], axis=0
    )
    product = dot_tn(source, jnp.concatenate([ref[...] for ref in d_values], axis=0))
    out_ref[...] = product.reshape(chips, rows, width).astype(out_ref.dtype)


def weight_call(blocks, d_values, other, owners, dtype, after=()):
    shape = (owners // 2, blocks[0].shape[1] // owners, d_values[0].shape[1])
    kernel = functools.partial(weight_kernel, len(blocks), other, owners)
    in_specs = [VMEM] * (2 * len(blocks)) + [pl.BlockSpec(memory_space=pl.ANY)] * len(after)
    return call(kernel, [struct(shape, dtype)], 1_000_000_000, (*blocks, *d_values, *after), in_specs)[0]


def swap(array, axis, distance):
    size = lax.axis_size(axis)
    return lax.ppermute(array, axis, [(i, i ^ distance) for i in range(size)])


def per_device(inputs, queries, keys, attention_gradient, value_matrix):
    nodes, owners = lax.axis_size("node"), lax.axis_size("dp")
    owner = lax.axis_index("dp")
    width = inputs.shape[1] // nodes

    packed = pack_call(inputs, nodes)
    blocks = [packed[0]] + [swap(packed[k], "node", k) for k in range(1, nodes)]
    d_values, attention = softmax_call(queries, keys, attention_gradient)
    all_d_values = [d_values] + [swap(d_values, "node", k) for k in range(1, nodes)]
    parts = values_call(blocks, value_matrix)
    values = [parts[0]] + [swap(parts[k], "node", k) for k in range(1, nodes)]
    key_gradient = key_call(queries, attention_gradient, attention, values)

    rows = width // owners
    if rows % 16 or owners % 2:
        local = dot_tn(jnp.concatenate(blocks, axis=0), jnp.concatenate(all_d_values, axis=0))
        owned = lax.psum_scatter(local, "dp", scatter_dimension=0, tiled=True)
        return key_gradient, owned / (owners * nodes)
    chip, chips = owner // 2, owners // 2
    send = weight_call(blocks, all_d_values, 1, owners, jnp.bfloat16, (parts[0],))
    keep = weight_call(blocks, all_d_values, 0, owners, jnp.float32)
    pair = keep + swap(send, "dp", 1).astype(jnp.float32)

    def chip_rows(other):
        return lax.dynamic_index_in_dim(pair, other, axis=0, keepdims=False)

    owned = chip_rows(chip)
    for k in range(1, chips):
        owned += swap(chip_rows(chip ^ k).astype(jnp.bfloat16), "dp", 2 * k).astype(jnp.float32)
    return key_gradient, owned / (owners * nodes)


def solution(mesh):
    placed = (
        P(("dp", "node"), None),
        P(("dp", "node"), None),
        P(("dp", "node"), None),
        P(("dp", "node"), None),
        P("node", None),
    )
    return jax.shard_map(
        per_device,
        mesh=mesh,
        in_specs=placed,
        out_specs=(P(("dp", "node"), None), P(("node", "dp"), None)),
        check_vma=False,
    )
```

```python
import functools

import jax
import jax.numpy as jnp
from jax import lax
from jax.experimental import pallas as pl
from jax.experimental.pallas import tpu as pltpu
from jax.sharding import PartitionSpec as P

QUERY_HEADS = 32
KEY_VALUE_HEADS = 4
HEAD_SIZE = 128
GROUP = QUERY_HEADS // KEY_VALUE_HEADS
FACTOR = HEAD_SIZE ** (-0.5)
LOG2_E = 1.4426950408889634
VMEM = pl.BlockSpec(memory_space=pltpu.VMEM)


def dot(a, b):
    return jnp.dot(a, b, preferred_element_type=jnp.float32)


def dot_nt(a, b):
    return lax.dot_general(a, b, (((1,), (1,)), ((), ())), preferred_element_type=jnp.float32)


def dot_tn(a, b):
    return lax.dot_general(a, b, (((0,), (0,)), ((), ())), preferred_element_type=jnp.float32)


def head(ref, h):
    return ref[:, h * HEAD_SIZE : (h + 1) * HEAD_SIZE]


def stack(ref, first, count):
    return jnp.concatenate([head(ref, first + i) for i in range(count)], axis=0)


def call(kernel, out_shape, flops, arguments, in_specs=None, scratch=()):
    return pl.pallas_call(
        kernel,
        in_specs=in_specs or [VMEM] * len(arguments),
        out_specs=[VMEM] * len(out_shape),
        out_shape=out_shape,
        scratch_shapes=scratch,
        compiler_params=pltpu.CompilerParams(vmem_limit_bytes=40 << 20),
        cost_estimate=pl.CostEstimate(flops=flops, bytes_accessed=1_000_000, transcendentals=0),
    )(*arguments)


def struct(shape, dtype):
    return jax.ShapeDtypeStruct(shape, dtype)


def pack_kernel(nodes, source_ref, *refs):
    outs, sems = refs[:nodes], refs[nodes]
    node = lax.axis_index("node")
    width = outs[0].shape[1]
    copies = []
    for k in (*range(1, nodes), 0):
        columns = pl.ds(pl.multiple_of((node ^ k) * width, width), width)
        copies.append(pltpu.make_async_copy(source_ref.at[:, columns], outs[k], sems.at[k]))
        copies[-1].start()
    for copy in copies:
        copy.wait()


def pack_call(inputs, nodes):
    shape = (inputs.shape[0], inputs.shape[1] // nodes)
    return call(
        functools.partial(pack_kernel, nodes),
        [struct(shape, inputs.dtype)] * nodes,
        500_000_000,
        (inputs,),
        [pl.BlockSpec(memory_space=pl.ANY)],
        [pltpu.SemaphoreType.DMA((nodes,))],
    )


def softmax_kernel(q_ref, k_ref, g_ref, dv_ref, p_ref):
    tokens = q_ref.shape[0]
    wide = (tokens, GROUP * tokens)
    query = lax.broadcasted_iota(jnp.int32, wide, 1) % tokens
    seen = lax.broadcasted_iota(jnp.int32, wide, 0) <= query
    for g in range(KEY_VALUE_HEADS):
        scores = jnp.where(seen, dot_nt(head(k_ref, g), stack(q_ref, g * GROUP, GROUP)), -1e30)
        exponent = jnp.exp2((scores - jnp.max(scores, axis=0, keepdims=True)) * (FACTOR * LOG2_E))
        attention = exponent * (1.0 / jnp.sum(exponent, axis=0, keepdims=True))
        p_ref[:, g * wide[1] : (g + 1) * wide[1]] = attention
        d_values = dot(attention.astype(jnp.bfloat16), stack(g_ref, g * GROUP, GROUP))
        dv_ref[:, g * HEAD_SIZE : (g + 1) * HEAD_SIZE] = d_values.astype(jnp.bfloat16)


def softmax_call(queries, keys, gradient):
    tokens = queries.shape[0]
    outs = [struct(keys.shape, jnp.bfloat16), struct((tokens, QUERY_HEADS * tokens), jnp.float32)]
    return call(softmax_kernel, outs, 3000000000, (queries, keys, gradient))


def key_kernel(q_ref, g_ref, p_ref, *rest):
    value_refs, out_ref = rest[:-1], rest[-1]
    wide = GROUP * q_ref.shape[0]
    for g in range(KEY_VALUE_HEADS):
        value = sum(head(ref, g).astype(jnp.float32) for ref in value_refs).astype(jnp.bfloat16)
        attention = p_ref[:, g * wide : (g + 1) * wide]
        d_attention = dot_nt(value, stack(g_ref, g * GROUP, GROUP))
        row_dots = jnp.sum(attention * d_attention, axis=0, keepdims=True)
        d_scores = (attention * (d_attention - row_dots)).astype(jnp.bfloat16)
        gradient = dot(d_scores, stack(q_ref, g * GROUP, GROUP)) * FACTOR
        out_ref[:, g * HEAD_SIZE : (g + 1) * HEAD_SIZE] = gradient.astype(jnp.bfloat16)


def key_call(queries, gradient, attention, values):
    outs = [struct(values[0].shape, jnp.bfloat16)]
    return call(key_kernel, outs, 2_500_000_000, (queries, gradient, attention, *values))[0]


def values_kernel(*refs):
    n = len(refs) // 2
    weights = refs[n][...]
    for source, out in zip(refs[:n], refs[n + 1 :]):
        out[...] = dot(source[...], weights).astype(out.dtype)


def values_call(blocks, weights):
    n = len(blocks)
    shape = (blocks[0].shape[0], weights.shape[1])
    outs = [struct(shape, jnp.float32 if i == 0 else jnp.bfloat16) for i in range(n)]
    return call(values_kernel, outs, 1500000000, (*blocks, weights))


def weight_kernel(n, other, owners, *refs):
    blocks, d_values, out_ref = refs[:n], refs[n : 2 * n], refs[-1]
    chips, rows, width = out_ref.shape
    core = (lax.axis_index("dp") + other) % 2
    columns = [pl.ds(pl.multiple_of((2 * i + core) * rows, rows), rows) for i in range(chips)]
    source = jnp.concatenate(
        [jnp.concatenate([ref[:, c] for c in columns], axis=1) for ref in blocks], axis=0
    )
    product = dot_tn(source, jnp.concatenate([ref[...] for ref in d_values], axis=0))
    out_ref[...] = product.reshape(chips, rows, width).astype(out_ref.dtype)


def weight_call(blocks, d_values, other, owners, dtype, after=(), flops=1_000_000_000):
    shape = (owners // 2, blocks[0].shape[1] // owners, d_values[0].shape[1])
    kernel = functools.partial(weight_kernel, len(blocks), other, owners)
    in_specs = [VMEM] * (2 * len(blocks)) + [pl.BlockSpec(memory_space=pl.ANY)] * len(after)
    return call(kernel, [struct(shape, dtype)], flops, (*blocks, *d_values, *after), in_specs)[0]


def swap(array, axis, distance):
    size = lax.axis_size(axis)
    return lax.ppermute(array, axis, [(i, i ^ distance) for i in range(size)])


def per_device(inputs, queries, keys, attention_gradient, value_matrix):
    nodes, owners = lax.axis_size("node"), lax.axis_size("dp")
    owner = lax.axis_index("dp")
    width = inputs.shape[1] // nodes

    packed = pack_call(inputs, nodes)
    blocks = [packed[0]] + [swap(packed[k], "node", k) for k in range(1, nodes)]
    order = [0, *range(nodes - 1, 0, -1)]
    d_values, attention = softmax_call(queries, keys, attention_gradient)
    all_d_values = [d_values] + [swap(d_values, "node", k) for k in range(1, nodes)]
    parts = values_call([blocks[k] for k in order], value_matrix)
    parts = [parts[order.index(k)] for k in range(nodes)]
    values = [parts[0]] + [swap(parts[k], "node", k) for k in range(1, nodes)]
    key_gradient = key_call(queries, attention_gradient, attention, values)

    rows = width // owners
    if rows % 16 or owners % 2:
        local = dot_tn(jnp.concatenate(blocks, axis=0), jnp.concatenate(all_d_values, axis=0))
        owned = lax.psum_scatter(local, "dp", scatter_dimension=0, tiled=True)
        return key_gradient, owned / (owners * nodes)
    chip, chips = owner // 2, owners // 2
    send = weight_call([blocks[k] for k in order], [all_d_values[k] for k in order], 1, owners, jnp.bfloat16, (parts[0],))
    keep = weight_call([blocks[k] for k in order], [all_d_values[k] for k in order], 0, owners, jnp.float32, (), 6000000000)
    pair = keep + swap(send, "dp", 1).astype(jnp.float32)

    def chip_rows(other):
        return lax.dynamic_index_in_dim(pair, other, axis=0, keepdims=False)

    owned = chip_rows(chip)
    for k in sorted(range(1, chips), key=lambda k: (k == chips - 1, k % 2)):
        owned += swap(chip_rows(chip ^ k).astype(jnp.bfloat16), "dp", 2 * k).astype(jnp.float32)
    return key_gradient, owned / (owners * nodes)


def solution(mesh):
    placed = (
        P(("dp", "node"), None),
        P(("dp", "node"), None),
        P(("dp", "node"), None),
        P(("dp", "node"), None),
        P("node", None),
    )
    return jax.shard_map(
        per_device,
        mesh=mesh,
        in_specs=placed,
        out_specs=(P(("dp", "node"), None), P(("node", "dp"), None)),
        check_vma=False,
    )
```

```python
import functools

import jax
import jax.numpy as jnp
from jax import lax
from jax.experimental import pallas as pl
from jax.experimental.pallas import tpu as pltpu
from jax.sharding import PartitionSpec as P

QUERY_HEADS = 32
KEY_VALUE_HEADS = 4
HEAD_SIZE = 128
GROUP = QUERY_HEADS // KEY_VALUE_HEADS
FACTOR = HEAD_SIZE ** (-0.5)
LOG2_E = 1.4426950408889634
VMEM = pl.BlockSpec(memory_space=pltpu.VMEM)


def dot(a, b):
    return jnp.dot(a, b, preferred_element_type=jnp.float32)


def dot_nt(a, b):
    return lax.dot_general(a, b, (((1,), (1,)), ((), ())), preferred_element_type=jnp.float32)


def dot_tn(a, b):
    return lax.dot_general(a, b, (((0,), (0,)), ((), ())), preferred_element_type=jnp.float32)


def head(ref, h):
    return ref[:, h * HEAD_SIZE : (h + 1) * HEAD_SIZE]


def stack(ref, first, count):
    return jnp.concatenate([head(ref, first + i) for i in range(count)], axis=0)


def call(kernel, out_shape, flops, arguments, in_specs=None, scratch=()):
    return pl.pallas_call(
        kernel,
        in_specs=in_specs or [VMEM] * len(arguments),
        out_specs=[VMEM] * len(out_shape),
        out_shape=out_shape,
        scratch_shapes=scratch,
        compiler_params=pltpu.CompilerParams(vmem_limit_bytes=40 << 20),
        cost_estimate=pl.CostEstimate(flops=flops, bytes_accessed=1_000_000, transcendentals=0),
    )(*arguments)


def struct(shape, dtype):
    return jax.ShapeDtypeStruct(shape, dtype)


def pack_kernel(nodes, source_ref, *refs):
    outs, sems = refs[:nodes], refs[nodes]
    node = lax.axis_index("node")
    width = outs[0].shape[1]
    copies = []
    for k in (*range(1, nodes), 0):
        columns = pl.ds(pl.multiple_of((node ^ k) * width, width), width)
        copies.append(pltpu.make_async_copy(source_ref.at[:, columns], outs[k], sems.at[k]))
        copies[-1].start()
    for copy in copies:
        copy.wait()


def pack_call(inputs, nodes):
    shape = (inputs.shape[0], inputs.shape[1] // nodes)
    return call(
        functools.partial(pack_kernel, nodes),
        [struct(shape, inputs.dtype)] * nodes,
        500_000_000,
        (inputs,),
        [pl.BlockSpec(memory_space=pl.ANY)],
        [pltpu.SemaphoreType.DMA((nodes,))],
    )


def softmax_kernel(q_ref, k_ref, g_ref, dv_ref, p_ref):
    tokens = q_ref.shape[0]
    wide = (tokens, GROUP * tokens)
    query = lax.broadcasted_iota(jnp.int32, wide, 1) % tokens
    seen = lax.broadcasted_iota(jnp.int32, wide, 0) <= query
    for g in range(KEY_VALUE_HEADS):
        scores = jnp.where(seen, dot_nt(head(k_ref, g), stack(q_ref, g * GROUP, GROUP)), -1e30)
        exponent = jnp.exp2((scores - jnp.max(scores, axis=0, keepdims=True)) * (FACTOR * LOG2_E))
        attention = exponent * (1.0 / jnp.sum(exponent, axis=0, keepdims=True))
        p_ref[:, g * wide[1] : (g + 1) * wide[1]] = attention
        d_values = dot(attention.astype(jnp.bfloat16), stack(g_ref, g * GROUP, GROUP))
        dv_ref[:, g * HEAD_SIZE : (g + 1) * HEAD_SIZE] = d_values.astype(jnp.bfloat16)


def softmax_call(queries, keys, gradient):
    tokens = queries.shape[0]
    outs = [struct(keys.shape, jnp.bfloat16), struct((tokens, QUERY_HEADS * tokens), jnp.float32)]
    return call(softmax_kernel, outs, 3000000000, (queries, keys, gradient))


def key_kernel(q_ref, g_ref, p_ref, *rest):
    value_refs, out_ref = rest[:-1], rest[-1]
    wide = GROUP * q_ref.shape[0]
    for g in range(KEY_VALUE_HEADS):
        value = sum(head(ref, g).astype(jnp.float32) for ref in value_refs).astype(jnp.bfloat16)
        attention = p_ref[:, g * wide : (g + 1) * wide]
        d_attention = dot_nt(value, stack(g_ref, g * GROUP, GROUP))
        row_dots = jnp.sum(attention * d_attention, axis=0, keepdims=True)
        d_scores = (attention * (d_attention - row_dots)).astype(jnp.bfloat16)
        gradient = dot(d_scores, stack(q_ref, g * GROUP, GROUP)) * FACTOR
        out_ref[:, g * HEAD_SIZE : (g + 1) * HEAD_SIZE] = gradient.astype(jnp.bfloat16)


def key_call(queries, gradient, attention, values):
    outs = [struct(values[0].shape, jnp.bfloat16)]
    return call(key_kernel, outs, 2_500_000_000, (queries, gradient, attention, *values))[0]


def values_kernel(n, *refs):
    weights = refs[n][...]
    for source, out in zip(refs[:n], refs[-n:]):
        out[...] = dot(source[...], weights).astype(out.dtype)


def values_call(blocks, weights, after=()):
    n = len(blocks)
    shape = (blocks[0].shape[0], weights.shape[1])
    outs = [struct(shape, jnp.float32 if i == 0 else jnp.bfloat16) for i in range(n)]
    kernel = functools.partial(values_kernel, n)
    in_specs = [VMEM] * (n + 1) + [pl.BlockSpec(memory_space=pl.ANY)] * len(after)
    return call(kernel, outs, 1_500_000_000, (*blocks, weights, *after), in_specs)


def weight_kernel(n, other, distances, *refs):
    blocks, d_values, out_ref = refs[:n], refs[n : 2 * n], refs[-1]
    _, rows, width = out_ref.shape
    owner = lax.axis_index("dp")
    core, chip = (owner + other) % 2, owner // 2
    starts = [(2 * (chip ^ k) + core) * rows for k in distances]
    columns = [pl.ds(pl.multiple_of(start, rows), rows) for start in starts]
    source = jnp.concatenate(
        [jnp.concatenate([ref[:, c] for c in columns], axis=1) for ref in blocks], axis=0
    )
    product = dot_tn(source, jnp.concatenate([ref[...] for ref in d_values], axis=0))
    out_ref[...] = product.reshape(len(distances), rows, width).astype(out_ref.dtype)


def weight_call(blocks, d_values, other, owners, distances, after=(), flops=500_000_000):
    dtype = jnp.bfloat16 if other else jnp.float32
    shape = (len(distances), blocks[0].shape[1] // owners, d_values[0].shape[1])
    kernel = functools.partial(weight_kernel, len(blocks), other, distances)
    in_specs = [VMEM] * (2 * len(blocks)) + [pl.BlockSpec(memory_space=pl.ANY)] * len(after)
    return call(kernel, [struct(shape, dtype)], flops, (*blocks, *d_values, *after), in_specs)[0]


def mark_kernel(*refs):
    refs[-1][...] = jnp.zeros_like(refs[-1])


def mark(arrays):
    in_specs = [pl.BlockSpec(memory_space=pl.ANY)] * len(arrays)
    return call(mark_kernel, [struct((8, 128), jnp.float32)], 100_000_000, arrays, in_specs)[0]


def swap(array, axis, distance):
    size = lax.axis_size(axis)
    return lax.ppermute(array, axis, [(i, i ^ distance) for i in range(size)])


def per_device(inputs, queries, keys, attention_gradient, value_matrix):
    nodes, owners = lax.axis_size("node"), lax.axis_size("dp")
    width = inputs.shape[1] // nodes

    packed = pack_call(inputs, nodes)
    blocks = [packed[0]] + [swap(packed[k], "node", k) for k in range(1, nodes)]
    order = [0, *range(nodes - 1, 0, -1)]
    d_values, attention = softmax_call(queries, keys, attention_gradient)
    all_d_values = [d_values] + [swap(d_values, "node", k) for k in range(1, nodes)]

    rows = width // owners
    if rows % 16 or owners % 4:
        parts = values_call([blocks[k] for k in order], value_matrix, ())
        parts = [parts[order.index(k)] for k in range(nodes)]
        values = [parts[0]] + [swap(parts[k], "node", k) for k in range(1, nodes)]
        key_gradient = key_call(queries, attention_gradient, attention, values)
        local = dot_tn(jnp.concatenate(blocks, axis=0), jnp.concatenate(all_d_values, axis=0))
        owned = lax.psum_scatter(local, "dp", scatter_dimension=0, tiled=True)
        return key_gradient, owned / (owners * nodes)
    chips = owners // 2
    ordered = [blocks[k] for k in order], [all_d_values[k] for k in order]
    low, wide = jnp.bfloat16, jnp.float32
    halves = tuple(range(chips // 2, chips)), tuple(range(chips // 2))
    tick = mark(blocks[1:])
    pairs, keeps = {}, ()
    for distances in halves:
        send = weight_call(*ordered, 1, owners, distances, (tick, *keeps))
        keep = weight_call(*ordered, 0, owners, distances, (), 500_000_000)
        keeps = (keep,)
        pair = keep + swap(send, "dp", 1).astype(wide)
        pairs.update((k, pair[i]) for i, k in enumerate(distances))

    parts = values_call([blocks[k] for k in order], value_matrix, (pairs[chips // 2],))
    parts = [parts[order.index(k)] for k in range(nodes)]
    values = [parts[0]] + [swap(parts[k], "node", k) for k in range(1, nodes)]
    key_gradient = key_call(queries, attention_gradient, attention, values)
    owned = pairs[0]
    if chips == 4:
        passed = pairs[2] + swap(pairs[3].astype(low), "dp", 2).astype(wide)
        owned += swap(pairs[1].astype(low), "dp", 2).astype(wide)
        owned += swap(passed.astype(low), "dp", 4).astype(wide)
    else:
        for k in range(1, chips):
            owned += swap(pairs[k].astype(low), "dp", 2 * k).astype(wide)
    return key_gradient, owned / (owners * nodes)


def solution(mesh):
    placed = (
        P(("dp", "node"), None),
        P(("dp", "node"), None),
        P(("dp", "node"), None),
        P(("dp", "node"), None),
        P("node", None),
    )
    return jax.shard_map(
        per_device,
        mesh=mesh,
        in_specs=placed,
        out_specs=(P(("dp", "node"), None), P(("node", "dp"), None)),
        check_vma=False,
    )
```

```python
import functools

import jax
import jax.numpy as jnp
from jax import lax
from jax.experimental import pallas as pl
from jax.experimental.pallas import tpu as pltpu
from jax.sharding import PartitionSpec as P

QUERY_HEADS = 32
KEY_VALUE_HEADS = 4
HEAD_SIZE = 128
GROUP = QUERY_HEADS // KEY_VALUE_HEADS
FACTOR = HEAD_SIZE ** (-0.5)
LOG2_E = 1.4426950408889634
VMEM = pl.BlockSpec(memory_space=pltpu.VMEM)


def dot(a, b):
    return jnp.dot(a, b, preferred_element_type=jnp.float32)


def dot_nt(a, b):
    return lax.dot_general(a, b, (((1,), (1,)), ((), ())), preferred_element_type=jnp.float32)


def dot_tn(a, b):
    return lax.dot_general(a, b, (((0,), (0,)), ((), ())), preferred_element_type=jnp.float32)


def head(ref, h):
    return ref[:, h * HEAD_SIZE : (h + 1) * HEAD_SIZE]


def stack(ref, first, count):
    return jnp.concatenate([head(ref, first + i) for i in range(count)], axis=0)


def call(kernel, out_shape, flops, arguments, in_specs=None, scratch=()):
    return pl.pallas_call(
        kernel,
        in_specs=in_specs or [VMEM] * len(arguments),
        out_specs=[VMEM] * len(out_shape),
        out_shape=out_shape,
        scratch_shapes=scratch,
        compiler_params=pltpu.CompilerParams(vmem_limit_bytes=40 << 20),
        cost_estimate=pl.CostEstimate(flops=flops, bytes_accessed=1_000_000, transcendentals=0),
    )(*arguments)


def struct(shape, dtype):
    return jax.ShapeDtypeStruct(shape, dtype)


def pack_kernel(nodes, source_ref, *refs):
    outs, sems = refs[:nodes], refs[nodes]
    node = lax.axis_index("node")
    width = outs[0].shape[1]
    copies = []
    for k in (*range(1, nodes), 0):
        columns = pl.ds(pl.multiple_of((node ^ k) * width, width), width)
        copies.append(pltpu.make_async_copy(source_ref.at[:, columns], outs[k], sems.at[k]))
        copies[-1].start()
    for copy in copies:
        copy.wait()


def pack_call(inputs, nodes):
    shape = (inputs.shape[0], inputs.shape[1] // nodes)
    return call(
        functools.partial(pack_kernel, nodes),
        [struct(shape, inputs.dtype)] * nodes,
        500_000_000,
        (inputs,),
        [pl.BlockSpec(memory_space=pl.ANY)],
        [pltpu.SemaphoreType.DMA((nodes,))],
    )


def softmax_kernel(q_ref, k_ref, g_ref, dv_ref, p_ref):
    tokens = q_ref.shape[0]
    wide = (tokens, GROUP * tokens)
    query = lax.broadcasted_iota(jnp.int32, wide, 1) % tokens
    seen = lax.broadcasted_iota(jnp.int32, wide, 0) <= query
    for g in range(KEY_VALUE_HEADS):
        scores = jnp.where(seen, dot_nt(head(k_ref, g), stack(q_ref, g * GROUP, GROUP)), -1e30)
        exponent = jnp.exp2((scores - jnp.max(scores, axis=0, keepdims=True)) * (FACTOR * LOG2_E))
        attention = exponent * (1.0 / jnp.sum(exponent, axis=0, keepdims=True))
        p_ref[:, g * wide[1] : (g + 1) * wide[1]] = attention
        d_values = dot(attention.astype(jnp.bfloat16), stack(g_ref, g * GROUP, GROUP))
        dv_ref[:, g * HEAD_SIZE : (g + 1) * HEAD_SIZE] = d_values.astype(jnp.bfloat16)


def softmax_call(queries, keys, gradient):
    tokens = queries.shape[0]
    outs = [struct(keys.shape, jnp.bfloat16), struct((tokens, QUERY_HEADS * tokens), jnp.float32)]
    return call(softmax_kernel, outs, 3000000000, (queries, keys, gradient))


def key_kernel(q_ref, g_ref, p_ref, *rest):
    value_refs, out_ref = rest[:-1], rest[-1]
    wide = GROUP * q_ref.shape[0]
    for g in range(KEY_VALUE_HEADS):
        value = sum(head(ref, g).astype(jnp.float32) for ref in value_refs).astype(jnp.bfloat16)
        attention = p_ref[:, g * wide : (g + 1) * wide]
        d_attention = dot_nt(value, stack(g_ref, g * GROUP, GROUP))
        row_dots = jnp.sum(attention * d_attention, axis=0, keepdims=True)
        d_scores = (attention * (d_attention - row_dots)).astype(jnp.bfloat16)
        gradient = dot(d_scores, stack(q_ref, g * GROUP, GROUP)) * FACTOR
        out_ref[:, g * HEAD_SIZE : (g + 1) * HEAD_SIZE] = gradient.astype(jnp.bfloat16)


def key_call(queries, gradient, attention, values):
    outs = [struct(values[0].shape, jnp.bfloat16)]
    return call(key_kernel, outs, 2_500_000_000, (queries, gradient, attention, *values))[0]


def values_kernel(n, *refs):
    weights = refs[n][...]
    for source, out in zip(refs[:n], refs[-n:]):
        out[...] = dot(source[...], weights).astype(out.dtype)


def values_call(blocks, weights, after=()):
    n = len(blocks)
    shape = (blocks[0].shape[0], weights.shape[1])
    outs = [struct(shape, jnp.float32 if i == 0 else jnp.bfloat16) for i in range(n)]
    kernel = functools.partial(values_kernel, n)
    in_specs = [VMEM] * (n + 1) + [pl.BlockSpec(memory_space=pl.ANY)] * len(after)
    return call(kernel, outs, 1_500_000_000, (*blocks, weights, *after), in_specs)


def weight_kernel(n, other, distances, *refs):
    blocks, d_values, out_ref = refs[:n], refs[n : 2 * n], refs[-1]
    _, rows, width = out_ref.shape
    owner = lax.axis_index("dp")
    core, chip = (owner + other) % 2, owner // 2
    starts = [(2 * (chip ^ k) + core) * rows for k in distances]
    columns = [pl.ds(pl.multiple_of(start, rows), rows) for start in starts]
    source = jnp.concatenate(
        [jnp.concatenate([ref[:, c] for c in columns], axis=1) for ref in blocks], axis=0
    )
    product = dot_tn(source, jnp.concatenate([ref[...] for ref in d_values], axis=0))
    out_ref[...] = product.reshape(len(distances), rows, width).astype(out_ref.dtype)


def weight_call(blocks, d_values, other, owners, distances, after=(), flops=500_000_000):
    dtype = jnp.bfloat16 if other else jnp.float32
    shape = (len(distances), blocks[0].shape[1] // owners, d_values[0].shape[1])
    kernel = functools.partial(weight_kernel, len(blocks), other, distances)
    in_specs = [VMEM] * (2 * len(blocks)) + [pl.BlockSpec(memory_space=pl.ANY)] * len(after)
    return call(kernel, [struct(shape, dtype)], flops, (*blocks, *d_values, *after), in_specs)[0]


def copy_kernel(n, *refs):
    for source, out in zip(refs[:n], refs[-n:]):
        out[...] = source[...]


def copies_after(arrays, after):
    n = len(arrays)
    in_specs = [VMEM] * n + [pl.BlockSpec(memory_space=pl.ANY)] * len(after)
    outs = [struct(array.shape, array.dtype) for array in arrays]
    return call(functools.partial(copy_kernel, n), outs, 100_000_000, (*arrays, *after), in_specs)


def swap(array, axis, distance):
    size = lax.axis_size(axis)
    return lax.ppermute(array, axis, [(i, i ^ distance) for i in range(size)])


def per_device(inputs, queries, keys, attention_gradient, value_matrix):
    nodes, owners = lax.axis_size("node"), lax.axis_size("dp")
    width = inputs.shape[1] // nodes

    packed = pack_call(inputs, nodes)
    blocks = [packed[0]] + [swap(packed[k], "node", k) for k in range(1, nodes)]
    order = [0, *range(nodes - 1, 0, -1)]
    d_values, attention = softmax_call(queries, keys, attention_gradient)
    all_d_values = [d_values] + [swap(d_values, "node", k) for k in range(1, nodes)]

    rows = width // owners
    if rows % 16 or owners % 4:
        parts = values_call([blocks[k] for k in order], value_matrix, ())
        parts = [parts[order.index(k)] for k in range(nodes)]
        values = [parts[0]] + [swap(parts[k], "node", k) for k in range(1, nodes)]
        key_gradient = key_call(queries, attention_gradient, attention, values)
        local = dot_tn(jnp.concatenate(blocks, axis=0), jnp.concatenate(all_d_values, axis=0))
        owned = lax.psum_scatter(local, "dp", scatter_dimension=0, tiled=True)
        return key_gradient, owned / (owners * nodes)
    chips = owners // 2
    ordered = [blocks[k] for k in order], [all_d_values[k] for k in order]
    low, wide = jnp.bfloat16, jnp.float32
    halves = tuple(range(chips // 2, chips)), tuple(range(chips // 2))
    parts = values_call([blocks[k] for k in order], value_matrix)
    parts = [parts[order.index(k)] for k in range(nodes)]
    pairs, keeps = {}, ()
    for distances in halves:
        send = weight_call(*ordered, 1, owners, distances, (parts[0], *keeps))
        keep = weight_call(*ordered, 0, owners, distances, (), 500_000_000)
        keeps = (keep,)
        pair = keep + swap(send, "dp", 1).astype(wide)
        pairs.update((k, pair[i]) for i, k in enumerate(distances))

    parts[1:] = copies_after(parts[1:], (pairs[chips // 2],))
    values = [parts[0]] + [swap(parts[k], "node", k) for k in range(1, nodes)]
    key_gradient = key_call(queries, attention_gradient, attention, values)
    owned = pairs[0]
    if chips == 4:
        passed = pairs[2] + swap(pairs[3].astype(low), "dp", 2).astype(wide)
        owned += swap(pairs[1].astype(low), "dp", 2).astype(wide)
        owned += swap(passed.astype(low), "dp", 4).astype(wide)
    else:
        for k in range(1, chips):
            owned += swap(pairs[k].astype(low), "dp", 2 * k).astype(wide)
    return key_gradient, owned / (owners * nodes)


def solution(mesh):
    placed = (
        P(("dp", "node"), None),
        P(("dp", "node"), None),
        P(("dp", "node"), None),
        P(("dp", "node"), None),
        P("node", None),
    )
    return jax.shard_map(
        per_device,
        mesh=mesh,
        in_specs=placed,
        out_specs=(P(("dp", "node"), None), P(("node", "dp"), None)),
        check_vma=False,
    )
```
